32 devices in a mesh: rep: 4 (over z), tp: 8 (over y, x, core).
Axes of the slice: x: 2, y: 2, z: 4, core: 2. Of those that a mesh axis runs over, the one named last changes fastest.
Arguments:
- hidden: bfloat16 [2048, 4096], P(('rep', 'tp')), may hold values from -6 to 6
- norm_gain: bfloat16 [4096], replicated, may hold values from 0.5 to 1.5
- w_query: bfloat16 [4096, 1024], P(None, 'tp')
- w_key: bfloat16 [4096, 1024], P(None, 'tp'), as said below
- w_value: bfloat16 [4096, 1024], P(None, 'tp'), as said below
- w_output: bfloat16 [4096, 1024], P(None, 'tp'), may hold values from -0.1875 to 0.1875
- kv_pool: bfloat16 [64, 64, 2048], P('rep', None, 'tp'), as said below
- page_table: int32 [32, 2], P('rep'), may hold values from 0 to 15, as said below
- cache_len: int32 [32], P('rep'), may hold values from 1 to 128, as said below
- parents: int32 [32, 64], P('rep'), may hold values from -1 to 62, as said below
- depths: int32 [32, 64], P('rep'), may hold values from 0 to 63, as said below
- accept_node: int32 [32], P('rep'), may hold values from 0 to 63
- migrate_to: int32 [4], replicated, may hold values from 0 to 3, as said below
- leave_slot: int32 [4], replicated, may hold values from 0 to 7
Outputs:
- layer_out: bfloat16 [2048, 4096], P(('rep', 'tp'))
- accepted_kv: bfloat16 [32, 64, 2048], P('rep', None, 'tp')
The draws below stay inside these ranges and needn't reach their ends.
Inputs may be any that keep to these rules, and one draw needn't show every extreme that they name: `page_table`: each group's rows list each of its 16 pages once. `cache_len`: in each group some slot holds exactly 128 tokens. parents[r, i] < i; node 0 is the root with parent -1. `depths`: the depth of each node in its tree. `migrate_to`: A permutation of the groups that forms one cycle through all of them. `w_key`: the columns of the 4 query heads of one key-value head are equal. `w_value`: the columns of the 4 query heads of one key-value head are equal. `kv_pool`: the 4 heads of one key-value head hold equal keys and values.
All inputs are finite; a program needn't handle non-finite values.
Results may differ from the reference program's by a relative error of at most 0.022.
Values may be sent and summed in bfloat16 or wider, within the bound.
A program may use at most 64 MiB of HBM per device.

```python
import math
import jax
import jax.numpy as jnp
from jax import lax

D = 4096
HD = 128
GROUP = 4
DRAFT = 64
PAGE = 64
REQ_DEV = 8
PAGES_REQ = 2
HEADS = 8
CACHE = 128
POOL_DEV = 16
ROWS = 512
REQS = 32
N_REP = 4


def draw_w_query(key, part):
    base = jnp.clip(jax.random.normal(jax.random.fold_in(key, 21), (D, HEADS, HD), jnp.float32), -6.0, 6.0)
    strength = jnp.exp(jax.random.uniform(jax.random.fold_in(key, 22), (HEADS,), jnp.float32, math.log(16.0), math.log(96.0)))
    picks = jax.random.randint(jax.random.fold_in(key, 23), (HEADS,), 0, 4, dtype=jnp.int32)
    first = jax.random.randint(jax.random.fold_in(key, 24), (), 0, HEADS, dtype=jnp.int32)
    head_ids = jnp.arange(HEADS, dtype=jnp.int32)
    loud = (picks == 0) | (head_ids == first)
    loud = loud & (head_ids != (first + 1) % HEADS)
    strength = jnp.where(head_ids == first, 96.0, strength)
    factor = jnp.where(loud, strength, 1.0)
    drawn = base * factor[None, :, None] * D ** (-0.5)
    return drawn.reshape(D, HEADS * HD).astype(jnp.bfloat16)


def grouped_columns(key, salt):
    drawn = jax.random.normal(jax.random.fold_in(key, salt), (D, HEADS // GROUP, 1, HD), jnp.float32) * D ** (-0.5)
    drawn = drawn.astype(jnp.bfloat16)
    return jnp.broadcast_to(drawn, (D, HEADS // GROUP, GROUP, HD)).reshape(D, HEADS * HD)


def draw_w_key(key, part):
    return grouped_columns(key, 11)


def draw_w_value(key, part):
    return grouped_columns(key, 12)


def draw_kv_pool(key, part):
    drawn = jax.random.normal(jax.random.fold_in(key, 13), (N_REP * POOL_DEV, PAGE, HEADS // GROUP, 1, 2 * HD), jnp.float32)
    drawn = drawn.astype(jnp.bfloat16)
    return jnp.broadcast_to(drawn, (N_REP * POOL_DEV, PAGE, HEADS // GROUP, GROUP, 2 * HD)).reshape(N_REP * POOL_DEV, PAGE, HEADS * 2 * HD)


def draw_page_table(key, part):
    keys_all = jax.random.split(jax.random.fold_in(key, 14), N_REP)
    orders = jax.vmap(lambda one_key: jax.random.permutation(one_key, POOL_DEV))(keys_all)
    return orders.astype(jnp.int32).reshape(N_REP * REQ_DEV, PAGES_REQ)


def draw_cache_len(key, part):
    lengths = jax.random.randint(jax.random.fold_in(key, 16), (N_REP, REQ_DEV), 1, CACHE + 1, dtype=jnp.int32)
    chosen = jax.random.randint(jax.random.fold_in(key, 17), (N_REP, 1), 0, REQ_DEV, dtype=jnp.int32)
    slots = jnp.arange(REQ_DEV, dtype=jnp.int32)[None, :]
    return jnp.where(slots == chosen, CACHE, lengths).astype(jnp.int32).reshape(N_REP * REQ_DEV)


def draw_migrate_to(key, part):
    groups = jnp.arange(N_REP, dtype=jnp.int32)
    start = jax.random.randint(jax.random.fold_in(key, 31), (), 0, N_REP, dtype=jnp.int32)
    half = N_REP // 2
    leading = jnp.stack([start, (start + 1) % N_REP, (start + 1 + half) % N_REP, (start + half) % N_REP]).astype(jnp.int32)
    shuffled = jax.random.permutation(jax.random.fold_in(key, 32), N_REP).astype(jnp.int32)
    is_leading = jnp.any(groups[:, None] == leading[None, :], axis=1)
    lead_rank = jnp.sum(jnp.where(groups[:, None] == leading[None, :], jnp.arange(4, dtype=jnp.int32)[None, :], 0), axis=1)
    score = jnp.where(is_leading, lead_rank, shuffled + 4).astype(jnp.int32)
    order = jnp.argsort(score, stable=True).astype(jnp.int32)
    following = jnp.roll(order, -1)
    return jnp.zeros((N_REP,), jnp.int32).at[order].set(following).astype(jnp.int32)


def tree_draw(key):
    nodes = jnp.arange(DRAFT, dtype=jnp.int32)
    raw_bits = jax.random.randint(jax.random.fold_in(key, 15), (N_REP * REQ_DEV, DRAFT), 0, 1 << 30, dtype=jnp.int32)
    random_parents = raw_bits % jnp.maximum(nodes, 1)[None, :]
    rows = jnp.arange(N_REP * REQ_DEV, dtype=jnp.int32)[:, None]
    chain_parents = jnp.broadcast_to(nodes[None, :] - 1, (N_REP * REQ_DEV, DRAFT))
    picked = jnp.where(rows == 0, chain_parents, random_parents)
    tree_parents = jnp.where(nodes[None, :] > 0, picked, -1).astype(jnp.int32)

    def step_down(index, depth_now):
        column = lax.dynamic_index_in_dim(tree_parents, index, 1, keepdims=False)
        above = jnp.take_along_axis(depth_now, jnp.maximum(column, 0)[:, None], axis=1)[:, 0]
        value = jnp.where(index == 0, 0, above + 1).astype(jnp.int32)
        return lax.dynamic_update_index_in_dim(depth_now, value[:, None], index, 1)
    tree_depths = lax.fori_loop(0, DRAFT, step_down, jnp.zeros((N_REP * REQ_DEV, DRAFT), jnp.int32))
    return (tree_parents, tree_depths)


def draw_parents(key, part):
    return tree_draw(key)[0]


def draw_depths(key, part):
    return tree_draw(key)[1]


def place_ends(values, rng, least, high):
    spot = [jax.random.randint(jax.random.fold_in(rng, axis), (), 0, length) for axis, length in enumerate(values.shape)]
    main_axis = values.shape.index(max(values.shape))
    next_to = spot[:main_axis] + [(spot[main_axis] + 1) % values.shape[main_axis]] + spot[main_axis + 1:]
    return values.at[tuple(spot)].set(least).at[tuple(next_to)].set(high)


def block_levels(rng, shape, pieces, smallest, high):
    loudness, own = 1.0, jax.random.fold_in(rng, 6)
    for axis_at, shards_of in pieces:
        steps = jnp.exp(jax.random.uniform(jax.random.fold_in(own, axis_at), (shards_of,), jnp.float32, smallest / len(pieces), high / len(pieces)))
        loudness = loudness * jnp.repeat(steps, shape[axis_at] // shards_of).reshape([-1 if axis == axis_at else 1 for axis in range(len(shape))])
    return loudness


def centred(stream_key, dims, deviation, most, pieces=(), kind=jnp.bfloat16):
    result = deviation * jax.random.normal(stream_key, dims, jnp.float32)
    if pieces:
        result = result * block_levels(stream_key, dims, pieces, -0.22, 0.18)
    return jnp.clip(result, -most, most).astype(kind)


def setup_inputs(seed: int = 0) -> dict:
    splits = jax.random.split(jax.random.key(seed), 15)
    return {
        "hidden": centred(splits[0], (N_REP * ROWS, D), 1.0, 6.0, ((0, 32),)),
        "norm_gain": jnp.clip(1.0 + 0.1 * jax.random.normal(splits[1], (D,), jnp.float32), 0.5, 1.5).astype(jnp.bfloat16),
        "w_query": draw_w_query(jax.random.fold_in(splits[14], 71), 0),
        "w_key": draw_w_key(jax.random.fold_in(splits[14], 71), 0),
        "w_value": draw_w_value(jax.random.fold_in(splits[14], 71), 0),
        "w_output": centred(splits[5], (D, HEADS * HD), (HEADS * HD) ** -0.5, 0.1875, ((1, 8),)),
        "kv_pool": draw_kv_pool(jax.random.fold_in(splits[14], 71), 0),
        "page_table": draw_page_table(jax.random.fold_in(splits[14], 71), 0),
        "cache_len": draw_cache_len(jax.random.fold_in(splits[14], 71), 0),
        "parents": draw_parents(jax.random.fold_in(splits[14], 71), 0),
        "depths": draw_depths(jax.random.fold_in(splits[14], 71), 0),
        "accept_node": place_ends(jax.random.randint(splits[11], (REQS,), 0, DRAFT), jax.random.fold_in(splits[11], 1), 0, DRAFT - 1).astype(jnp.int32),
        "migrate_to": draw_migrate_to(jax.random.fold_in(splits[14], 71), 0),
        "leave_slot": place_ends(jax.random.randint(splits[13], (N_REP,), 0, REQ_DEV), jax.random.fold_in(splits[13], 1), 0, REQ_DEV - 1).astype(jnp.int32),
    }


eps = 1e-05
rope_base = 1000000.0

def rotate(values_in, positions):
    half = values_in.shape[-1] // 2
    freq = rope_base ** (-(jnp.arange(half, dtype=jnp.float32) * 2.0 / values_in.shape[-1]))
    angle = positions.astype(jnp.float32)[:, None] * freq[None, :]
    cosine = jnp.cos(angle)[:, None, :]
    sine = jnp.sin(angle)[:, None, :]
    first = values_in[..., :half]
    second = values_in[..., half:]
    return jnp.concatenate([first * cosine - second * sine, second * cosine + first * sine], axis=-1)

def ancestors(parents):
    count = parents.shape[-1]
    nodes = jnp.arange(count, dtype=jnp.int32)
    step_up = (parents[..., :, None] == nodes).astype(jnp.float32)
    reach = jnp.eye(count, dtype=jnp.float32) + step_up
    for sweep in range(max(1, (count - 1).bit_length())):
        reach = jnp.minimum(jnp.einsum('rij,rjk->rik', reach, reach, precision=lax.Precision.HIGHEST), 1.0)
    return reach

def head_terms(query, keys, values, allowed):
    scale = 1.0 / math.sqrt(query.shape[-1])
    scores = jnp.einsum('qhd,khd->hqk', query.astype(jnp.float32), keys.astype(jnp.float32)) * scale
    scores = jnp.where(allowed[None], scores, -1e+30)
    peak = lax.optimization_barrier(jnp.max(scores, axis=-1))
    weights = jnp.exp(scores - peak[..., None])
    total = lax.optimization_barrier(jnp.sum(weights, axis=-1))
    rounded = weights.astype(jnp.bfloat16).astype(jnp.float32)
    summed = jnp.einsum('hqk,khd->hqd', rounded, values.astype(jnp.float32))
    return (peak, total, summed)

def merged(peak_one, total_one, summed_one, peak_two, total_two, summed_two):
    peak = jnp.maximum(peak_one, peak_two)
    scale_one = jnp.exp(peak_one - peak)
    scale_two = jnp.exp(peak_two - peak)
    upper = summed_one * scale_one[..., None] + summed_two * scale_two[..., None]
    lower = total_one * scale_one + total_two * scale_two
    return upper / lower[..., None]

def reference(hidden, norm_gain, w_query, w_key, w_value, w_output, kv_pool, page_table, cache_len, parents, depths, accept_node, migrate_to, leave_slot):
    residual = hidden.astype(jnp.float32)
    normed = (residual * lax.rsqrt(lax.optimization_barrier(jnp.mean(residual * residual, axis=-1, keepdims=True)) + eps) * norm_gain.astype(jnp.float32)).astype(jnp.bfloat16)
    count = normed.shape[0]
    query = jnp.dot(normed, w_query, preferred_element_type=jnp.float32).reshape(count, HEADS, HD)
    keys_new = jnp.dot(normed, w_key, preferred_element_type=jnp.float32).reshape(count, HEADS, HD)
    values_new = jnp.dot(normed, w_value, preferred_element_type=jnp.float32).reshape(count, HEADS, HD)
    groups = jnp.arange(N_REP, dtype=jnp.int32)
    source_of = jnp.zeros((N_REP,), jnp.int32).at[migrate_to].set(groups)
    slot_group = jnp.repeat(groups, REQ_DEV)
    slot_local = jnp.tile(jnp.arange(REQ_DEV, dtype=jnp.int32), N_REP)
    arriving = slot_local == leave_slot[slot_group]
    old_group = jnp.where(arriving, source_of[slot_group], slot_group).astype(jnp.int32)
    old_local = jnp.where(arriving, leave_slot[source_of[slot_group]], slot_local).astype(jnp.int32)
    old_index = old_group * REQ_DEV + old_local
    old_len = cache_len[old_index]
    pages = page_table[old_index] + (old_group * POOL_DEV)[:, None]
    positions = (old_len[:, None] + depths).reshape(-1)
    q_rot = rotate(query, positions).astype(jnp.bfloat16).reshape(-1, DRAFT, HEADS, HD)
    k_rot = rotate(keys_new, positions).astype(jnp.bfloat16).reshape(-1, DRAFT, HEADS, HD)
    v_new = values_new.astype(jnp.bfloat16).reshape(-1, DRAFT, HEADS, HD)
    ancestry = ancestors(parents)

    def one_request(items):
        q_req, k_req, v_req, pages_req, len_req, tree_req = items
        cache = kv_pool[pages_req].reshape(CACHE, HEADS, 2 * HD)
        valid = jnp.arange(CACHE, dtype=jnp.int32) < len_req
        allowed = jnp.broadcast_to(valid[None, :], (DRAFT, CACHE))
        first = head_terms(q_req, cache[..., :HD], cache[..., HD:], allowed)
        second = head_terms(q_req, k_req, v_req, tree_req > 0.5)
        out = merged(first[0], first[1], first[2], second[0], second[1], second[2])
        return jnp.transpose(out, (1, 0, 2)).astype(jnp.bfloat16)
    attn = lax.map(one_request, (q_rot, k_rot, v_new, pages, old_len, ancestry)).reshape(count, HEADS, HD)
    out_heads = w_output.reshape(D, HEADS, HD)

    def head_step(total, head):
        attn_head = lax.dynamic_index_in_dim(attn, head, 1, keepdims=False)
        weight_head = lax.dynamic_index_in_dim(out_heads, head, 1, keepdims=False)
        term = lax.dot_general(attn_head, weight_head, (((1,), (1,)), ((), ())), preferred_element_type=jnp.float32)
        rounded = lax.optimization_barrier(term.astype(jnp.bfloat16))
        return (total + rounded.astype(jnp.float32), None)
    proj, unused = lax.scan(head_step, jnp.zeros((count, D), jnp.float32), jnp.arange(HEADS, dtype=jnp.int32))
    layer_out = (residual + proj).astype(jnp.bfloat16)
    on_path = jnp.take_along_axis(ancestry, accept_node[:, None, None], axis=1)[:, 0, :]
    levels = jnp.arange(DRAFT, dtype=jnp.int32)
    select = on_path[:, None, :] * (depths[:, None, :] == levels[None, :, None]).astype(jnp.float32)
    kv_all = jnp.concatenate([k_rot, v_new], axis=-1).astype(jnp.float32)
    accepted = jnp.einsum('rji,rihc->rjhc', select, kv_all).astype(jnp.bfloat16)
    accepted_kv = accepted.reshape(-1, DRAFT, HEADS * 2 * HD)
    return (layer_out, accepted_kv)
```

```python
import functools
import math

import jax
import jax.numpy as jnp
from jax import lax
from jax.experimental import pallas as pl
from jax.experimental.pallas import tpu as pltpu
from jax.sharding import PartitionSpec as P

eps = 1e-05
rope_base = 1000000.0
MESH = pl.DeviceIdType.MESH
F32 = jnp.float32
BF16 = jnp.bfloat16


def kernel(
    n,
    reps,
    page_table,
    cache_len,
    accept,
    migrate_to,
    leave_slot,
    hidden,
    gain,
    pool,
    parent_col,
    depth_col,
    depth_row,
    freq,
    w_query,
    w_key,
    w_value,
    w_output,
    out,
    accepted,
    rows,
    w_qkv,
    w_out,
    pages,
    moved_len,
    new_len,
    cos_tab,
    sin_tab,
    anc_tab,
    terms,
    pair_in,
    pair_sum,
    rs_in,
    local_sem,
    ag_send,
    ag_recv,
    fw_send,
    fw_recv,
    ps_send,
    ps_recv,
    rs_send,
    rs_recv,
    mg_send,
    mg_recv,
    ml_send,
    ml_recv,
):
    chips = n // 2
    rows_dev, width = hidden.shape
    head = w_out.shape[1]
    slots = accept.shape[0]
    draft = rows.shape[0] // slots
    pair_rows = 2 * draft
    pairs = slots // 2
    pool_pages = pool.shape[0]
    rep = lax.axis_index("rep")
    me = lax.axis_index("tp")
    core = me % 2
    chip = me // 2
    sibling = chip * 2 + (1 - core)

    def dst_chip(d):
        if chips == 4:
            return ((chip // 2 + d // 2) % 2) * 2 + (chip % 2 + d % 2) % 2
        return (chip + d) % chips

    def src_chip(d):
        if chips == 4:
            return dst_chip(d)
        return (chip + chips - d) % chips

    def block(ref, dev):
        return ref.at[pl.ds(pl.multiple_of(dev * rows_dev, rows_dev), rows_dev), :]

    def remote(src, dst, send, recv, where):
        return pltpu.make_async_remote_copy(
            src_ref=src, dst_ref=dst, send_sem=send, recv_sem=recv,
            device_id=where, device_id_type=MESH,
        )

    loads = [
        pltpu.make_async_copy(w_query, w_qkv.at[:, pl.ds(0, head)], local_sem.at[0]),
        pltpu.make_async_copy(w_key, w_qkv.at[:, pl.ds(head, head)], local_sem.at[1]),
        pltpu.make_async_copy(w_value, w_qkv.at[:, pl.ds(2 * head, head)], local_sem.at[2]),
        pltpu.make_async_copy(w_output, w_out, local_sem.at[3]),
        pltpu.make_async_copy(pool, pages.at[pl.ds(0, pool_pages)], local_sem.at[4]),
    ]
    barrier = pltpu.get_barrier_semaphore()
    pl.semaphore_signal(barrier, inc=1, device_id={"tp": sibling}, device_id_type=MESH)
    for d in range(1, chips):
        pl.semaphore_signal(
            barrier, inc=1, device_id={"tp": dst_chip(d) * 2 + core}, device_id_type=MESH
        )
    for e in range(1, reps):
        pl.semaphore_signal(
            barrier, inc=1, device_id={"rep": (rep + e) % reps}, device_id_type=MESH
        )
    for load in loads:
        load.start()

    own = pl.multiple_of(me * rows_dev, rows_dev)

    @pl.loop(0, rows_dev // 16)
    def _(i):
        x = hidden[pl.ds(pl.multiple_of(i * 16, 16), 16), :].astype(F32)
        mean = jnp.mean(x * x, axis=-1, keepdims=True)
        y = x * lax.rsqrt(mean + eps) * gain[...].astype(F32)
        rows[pl.ds(pl.multiple_of(own + i * 16, 16), 16), :] = y.astype(BF16)

    leaving = leave_slot[rep]
    tail = pool_pages + 2 * rep
    pages[tail] = pool[page_table[leaving, 0]]
    pages[tail + 1] = pool[page_table[leaving, 1]]
    moved_len[rep] = jnp.full(moved_len.shape[1:], cache_len[leaving], jnp.int32)

    pl.semaphore_wait(barrier, 1 + (chips - 1) + (reps - 1))

    gathers = [
        remote(block(rows, me), block(rows, me), ag_send.at[0], ag_recv.at[0], {"tp": sibling})
    ]
    for d in range(1, chips):
        gathers.append(
            remote(
                block(rows, me), block(rows, me), ag_send.at[d], ag_recv.at[d],
                {"tp": dst_chip(d) * 2 + core},
            )
        )
    for d in list(range(1, chips)) + [0]:
        gathers[d].start()
    moves = []
    for e in range(1, reps):
        to = {"rep": (rep + e) % reps}
        moves.append(
            remote(moved_len.at[rep], moved_len.at[rep], ml_send.at[e], ml_recv.at[e], to)
        )
        moves.append(
            remote(
                pages.at[pl.ds(tail, 2)], pages.at[pl.ds(tail, 2)], mg_send.at[e],
                mg_recv.at[e], to,
            )
        )
    for move in moves:
        move.start()

    row_id = lax.broadcasted_iota(jnp.int32, (pair_rows, pair_rows), 0)
    col_id = lax.broadcasted_iota(jnp.int32, (pair_rows, pair_rows), 1)
    reach = []
    for p in range(pairs):
        above = parent_col[p * pair_rows : (p + 1) * pair_rows, :]
        reach.append(((col_id == above) | (col_id == row_id)).astype(F32))
    for sweep in range(max(1, (draft - 1).bit_length())):
        for p in range(pairs):
            low = reach[p].astype(BF16)
            reach[p] = jnp.minimum(jnp.dot(low, low, preferred_element_type=F32), 1.0)
    for p in range(pairs):
        anc_tab[p] = reach[p]

    for move in moves:
        move.wait()
    loads[4].wait()
    source = jnp.int32(0)
    for g in range(reps):
        source = jnp.where(migrate_to[g] == rep, g, source)
    came = moved_len[source][0:1, :]
    half_sign = jnp.where(
        lax.broadcasted_iota(jnp.int32, (1, head), 1) < head // 2, -1.0, 1.0
    ).astype(F32)
    for r in range(slots):
        is_new = (leaving == r).astype(jnp.int32)
        length = came * is_new + cache_len[r] * (1 - is_new)
        new_len[r] = length
        place = (length + depth_col[r * draft : (r + 1) * draft, :]).astype(F32)
        angle = place * freq[...]
        cos_tab[r * draft : (r + 1) * draft, :] = jnp.cos(angle)
        sin_tab[r * draft : (r + 1) * draft, :] = jnp.sin(angle) * half_sign
    for load in loads[:4]:
        load.wait()

    scale = 1.0 / math.sqrt(head)
    token = lax.broadcasted_iota(jnp.int32, (draft, 2 * pages.shape[1]), 1)
    forwards = []

    def arrive(d):
        gathers[d].wait_recv()
        held = block(rows, src_chip(d) * 2 + core)
        forward = remote(held, held, fw_send.at[d], fw_recv.at[d], {"tp": sibling})
        forward.start()
        forwards.append(forward)

    def attend(p):
        first_row = pl.multiple_of(p * pair_rows, pair_rows)
        span = pl.ds(first_row, pair_rows)
        qkv = jnp.dot(rows[span, :], w_qkv[...], preferred_element_type=F32)
        cos = cos_tab[span, :]
        sin = sin_tab[span, :]
        q = qkv[:, :head]
        k = qkv[:, head : 2 * head]
        q = (q * cos + pltpu.roll(q, head // 2, 1) * sin).astype(BF16)
        k = (k * cos + pltpu.roll(k, head // 2, 1) * sin).astype(BF16)
        v = qkv[:, 2 * head :].astype(BF16)
        ancestry = anc_tab[p]
        nt = (((1,), (1,)), ((), ()))
        tree = lax.dot_general(q, k, nt, preferred_element_type=F32) * scale
        tree = jnp.where(ancestry > 0.5, tree, -1e30)
        attn = []
        for part in range(2):
            r = 2 * p + part
            at = slice(part * draft, (part + 1) * draft)
            is_new = (leaving == r).astype(jnp.int32)
            cache = jnp.concatenate(
                [
                    pages[
                        page_table[r, j] * (1 - is_new)
                        + (pool_pages + 2 * source + j) * is_new
                    ]
                    for j in range(2)
                ],
                axis=0,
            )
            cached = lax.dot_general(
                q[at], cache[:, :head], nt, preferred_element_type=F32
            ) * scale
            cached = jnp.where(token < new_len[r], cached, -1e30)
            peak = jnp.maximum(
                jnp.max(cached, axis=-1, keepdims=True),
                jnp.max(tree[at], axis=-1, keepdims=True),
            )
            p_cache = jnp.exp(cached - peak)
            p_tree = jnp.exp(tree[at] - peak)
            total = jnp.sum(p_cache, axis=-1, keepdims=True) + jnp.sum(
                p_tree, axis=-1, keepdims=True
            )
            summed = jnp.dot(
                p_cache.astype(BF16), cache[:, head:], preferred_element_type=F32
            ) + jnp.dot(p_tree.astype(BF16), v, preferred_element_type=F32)
            attn.append((summed / total).astype(BF16))
        attn = jnp.concatenate(attn, axis=0)

        tile = 512

        @pl.loop(0, width // tile)
        def _(i):
            c = pl.ds(pl.multiple_of(i * tile, tile), tile)
            terms[span, c] = lax.dot_general(
                attn, w_out[c, :], nt, preferred_element_type=F32
            ).astype(BF16)

        return (p, k, v, ancestry)

    def accept_path(state):
        p, k, v, ancestry = state
        node = row_id[:, :1]
        chosen = ((node == accept[2 * p]) | (node == accept[2 * p + 1] + draft)).astype(F32)
        on_path = jnp.sum(ancestry * chosen, axis=0, keepdims=True)
        level = depth_row[p] + jnp.where(col_id[:1] < draft, 0, draft)
        select = jnp.where(level == row_id, on_path, 0.0).astype(BF16)
        got_k = jnp.dot(select, k, preferred_element_type=F32).astype(BF16)
        got_v = jnp.dot(select, v, preferred_element_type=F32).astype(BF16)
        for part in range(2):
            at = slice(part * draft, (part + 1) * draft)
            accepted[2 * p + part, :, :head] = got_k[at]
            accepted[2 * p + part, :, head:] = got_v[at]

    swaps = {}

    def swap(d):
        c = src_chip(d)
        swaps[d] = remote(
            block(terms, c * 2 + 1 - core), pair_in.at[c], ps_send.at[d], ps_recv.at[d],
            {"tp": sibling},
        )
        swaps[d].start()

    sends = []

    def pair_and_send(d):
        c = src_chip(d)
        swaps[d].wait_recv()
        base = (c * 2 + core) * rows_dev

        @pl.loop(0, rows_dev // 16)
        def _(i):
            mine = terms[pl.ds(pl.multiple_of(base + i * 16, 16), 16), :].astype(F32)
            at = pl.ds(pl.multiple_of(i * 16, 16), 16)
            pair_sum[c, at, :] = (mine + pair_in[c, at, :].astype(F32)).astype(BF16)

        send = remote(
            pair_sum.at[c], rs_in.at[d], rs_send.at[d], rs_recv.at[d], {"tp": c * 2 + core}
        )
        send.start()
        sends.append(send)

    if chips == pairs:
        gathers[0].wait_recv()
        state = attend(chip)
        swap(0)
        accept_path(state)
        for d in range(1, chips):
            arrive(d)
            forwards[-1].wait_recv()
            state = attend(src_chip(d))
            swap(d)
            accept_path(state)
            pair_and_send(d)
    else:
        gathers[0].wait_recv()
        for d in range(1, chips):
            arrive(d)
        for forward in forwards:
            forward.wait_recv()
        for p in range(pairs):
            accept_path(attend(p))
        for d in range(chips):
            swap(d)
        for d in range(1, chips):
            pair_and_send(d)

    swaps[0].wait_recv()
    for send in sends:
        send.wait_recv()

    @pl.loop(0, rows_dev // 16)
    def _(i):
        at = pl.ds(pl.multiple_of(i * 16, 16), 16)
        total = terms[pl.ds(pl.multiple_of(own + i * 16, 16), 16), :].astype(F32)
        total = total + pair_in[chip, at, :].astype(F32)
        for d in range(1, chips):
            total = total + rs_in[d, at, :].astype(F32)
        out[at, :] = (hidden[at, :].astype(F32) + total).astype(BF16)

    for copy in gathers + forwards + list(swaps.values()) + sends:
        copy.wait_send()


def local(
    n,
    reps,
    hidden,
    norm_gain,
    w_query,
    w_key,
    w_value,
    w_output,
    kv_pool,
    page_table,
    cache_len,
    parents,
    depths,
    accept_node,
    migrate_to,
    leave_slot,
):
    slots, draft = parents.shape
    rows_dev, width = hidden.shape
    head = w_query.shape[1]
    count = slots * draft
    chips = n // 2
    shift = (jnp.arange(slots, dtype=jnp.int32) % 2 * draft)[:, None]
    parent_col = jnp.where(parents >= 0, parents + shift, -1).reshape(count, 1)
    lane = jnp.arange(head, dtype=jnp.int32) % (head // 2)
    freq = (rope_base ** (-(lane.astype(F32) * 2.0 / head)))[None, :]
    smem = pl.BlockSpec(memory_space=pltpu.SMEM)
    vmem = pl.BlockSpec(memory_space=pltpu.VMEM)
    hbm = pl.BlockSpec(memory_space=pl.ANY)
    dma = pltpu.SemaphoreType.DMA
    page = kv_pool.shape[1]
    return pl.pallas_call(
        functools.partial(kernel, n, reps),
        out_shape=(
            jax.ShapeDtypeStruct((rows_dev, width), BF16),
            jax.ShapeDtypeStruct((slots, draft, 2 * head), BF16),
        ),
        in_specs=[smem] * 5 + [vmem] * 7 + [hbm] * 4,
        out_specs=(vmem, vmem),
        scratch_shapes=[
            pltpu.VMEM((count, width), BF16),
            pltpu.VMEM((width, 3 * head), BF16),
            pltpu.VMEM((width, head), BF16),
            pltpu.VMEM((kv_pool.shape[0] + 2 * reps, page, 2 * head), BF16),
            pltpu.VMEM((reps, 8, head), jnp.int32),
            pltpu.VMEM((slots, 1, head), jnp.int32),
            pltpu.VMEM((count, head), F32),
            pltpu.VMEM((count, head), F32),
            pltpu.VMEM((slots // 2, 2 * draft, 2 * draft), F32),
            pltpu.VMEM((count, width), BF16),
            pltpu.VMEM((chips, rows_dev, width), BF16),
            pltpu.VMEM((chips, rows_dev, width), BF16),
            pltpu.VMEM((chips, rows_dev, width), BF16),
            dma((5,)),
        ]
        + [dma((chips,))] * 8
        + [dma((reps,))] * 4,
        compiler_params=pltpu.CompilerParams(
            collective_id=0, has_side_effects=True, vmem_limit_bytes=48 * 1024 * 1024
        ),
    )(
        page_table,
        cache_len,
        accept_node,
        migrate_to,
        leave_slot,
        hidden,
        norm_gain[None, :],
        kv_pool,
        parent_col,
        depths.reshape(count, 1),
        depths.reshape(slots // 2, 1, 2 * draft),
        freq,
        w_query,
        w_key,
        w_value,
        w_output,
    )


def solution(mesh):
    in_specs = (
        P(("rep", "tp"), None),
        P(),
        P(None, "tp"),
        P(None, "tp"),
        P(None, "tp"),
        P(None, "tp"),
        P("rep", None, "tp"),
        P("rep", None),
        P("rep"),
        P("rep", None),
        P("rep", None),
        P("rep"),
        P(),
        P(),
    )
    out_specs = (P(("rep", "tp"), None), P("rep", None, "tp"))
    fn = functools.partial(local, mesh.shape["tp"], mesh.shape["rep"])
    return jax.shard_map(fn, mesh=mesh, in_specs=in_specs, out_specs=out_specs, check_vma=False)
```

```python
import functools
import math

import jax
import jax.numpy as jnp
from jax import lax
from jax.experimental import pallas as pl
from jax.experimental.pallas import tpu as pltpu
from jax.sharding import PartitionSpec as P

eps = 1e-05
rope_base = 1000000.0
MESH = pl.DeviceIdType.MESH
F32 = jnp.float32
BF16 = jnp.bfloat16


def kernel(
    n,
    reps,
    hidden,
    gain,
    pool,
    parents,
    depths,
    freq,
    page_table_in,
    cache_len_in,
    accept_in,
    migrate_to_in,
    leave_slot_in,
    w_query,
    w_key,
    w_value,
    w_output,
    out,
    accepted,
    rows,
    w_qkv,
    w_out,
    pages,
    moved_len,
    new_len,
    cos_tab,
    sin_tab,
    anc_tab,
    page_table,
    cache_len,
    accept,
    migrate_to,
    leave_slot,
    depth_row,
    terms,
    pair_in,
    pair_sum,
    rs_in,
    local_sem,
    ag_send,
    ag_recv,
    fw_send,
    fw_recv,
    ps_send,
    ps_recv,
    rs_send,
    rs_recv,
    mg_send,
    mg_recv,
    ml_send,
    ml_recv,
):
    chips = n // 2
    rows_dev, width = hidden.shape
    head = w_out.shape[1]
    slots = parents.shape[0]
    draft = rows.shape[0] // slots
    pair_rows = 2 * draft
    pairs = slots // 2
    pool_pages = pool.shape[0]
    rep = lax.axis_index("rep")
    me = lax.axis_index("tp")
    core = me % 2
    chip = me // 2
    sibling = chip * 2 + (1 - core)
    grid4 = chips == 4 and slots == 2 * chips
    first = 1 + core
    second = 2 - core

    def dst_chip(d):
        if chips == 4:
            return ((chip // 2 + d // 2) % 2) * 2 + (chip % 2 + d % 2) % 2
        return (chip + d) % chips

    def src_chip(d):
        if chips == 4:
            return dst_chip(d)
        return (chip + chips - d) % chips

    def block(ref, dev):
        return ref.at[pl.ds(pl.multiple_of(dev * rows_dev, rows_dev), rows_dev), :]

    def remote(src, dst, send, recv, where):
        return pltpu.make_async_remote_copy(
            src_ref=src, dst_ref=dst, send_sem=send, recv_sem=recv,
            device_id=where, device_id_type=MESH,
        )

    loads = [
        pltpu.make_async_copy(w_query, w_qkv.at[:, pl.ds(0, head)], local_sem.at[0]),
        pltpu.make_async_copy(w_key, w_qkv.at[:, pl.ds(head, head)], local_sem.at[1]),
        pltpu.make_async_copy(w_value, w_qkv.at[:, pl.ds(2 * head, head)], local_sem.at[2]),
        pltpu.make_async_copy(w_output, w_out, local_sem.at[3]),
        pltpu.make_async_copy(pool, pages.at[pl.ds(0, pool_pages)], local_sem.at[4]),
    ]
    small = [
        pltpu.make_async_copy(page_table_in, page_table, local_sem.at[5]),
        pltpu.make_async_copy(cache_len_in, cache_len, local_sem.at[6]),
        pltpu.make_async_copy(accept_in, accept, local_sem.at[7]),
        pltpu.make_async_copy(migrate_to_in, migrate_to, local_sem.at[8]),
        pltpu.make_async_copy(leave_slot_in, leave_slot, local_sem.at[9]),
    ]
    barrier = pltpu.get_barrier_semaphore()
    pl.semaphore_signal(barrier, inc=1, device_id={"tp": sibling}, device_id_type=MESH)
    for d in range(1, chips):
        pl.semaphore_signal(
            barrier, inc=1, device_id={"tp": dst_chip(d) * 2 + core}, device_id_type=MESH
        )
    for e in range(1, reps):
        pl.semaphore_signal(
            barrier, inc=1, device_id={"rep": (rep + e) % reps}, device_id_type=MESH
        )
    for load in small + loads:
        load.start()

    own = pl.multiple_of(me * rows_dev, rows_dev)

    @pl.loop(0, rows_dev // 16)
    def _(i):
        x = hidden[pl.ds(pl.multiple_of(i * 16, 16), 16), :].astype(F32)
        mean = jnp.mean(x * x, axis=-1, keepdims=True)
        y = x * lax.rsqrt(mean + eps) * gain[...].astype(F32)
        rows[pl.ds(pl.multiple_of(own + i * 16, 16), 16), :] = y.astype(BF16)

    for load in small:
        load.wait()
    leaving = leave_slot[rep]
    tail = pool_pages + 2 * rep
    pages[tail] = pool[page_table[leaving, 0]]
    pages[tail + 1] = pool[page_table[leaving, 1]]
    moved_len[rep] = jnp.full(moved_len.shape[1:], cache_len[leaving], jnp.int32)

    pl.semaphore_wait(barrier, 1 + (chips - 1) + (reps - 1))

    gathers = [
        remote(block(rows, me), block(rows, me), ag_send.at[0], ag_recv.at[0], {"tp": sibling})
    ]
    for d in range(1, 3 if grid4 else chips):
        way = (first if d == 1 else second) if grid4 else d
        gathers.append(
            remote(
                block(rows, me), block(rows, me), ag_send.at[d], ag_recv.at[d],
                {"tp": dst_chip(way) * 2 + core},
            )
        )
    for d in [1, 0] if grid4 else list(range(1, chips)) + [0]:
        gathers[d].start()
    moves = []
    for e in range(1, reps):
        to = {"rep": (rep + e) % reps}
        moves.append(
            remote(moved_len.at[rep], moved_len.at[rep], ml_send.at[e], ml_recv.at[e], to)
        )
        moves.append(
            remote(
                pages.at[pl.ds(tail, 2)], pages.at[pl.ds(tail, 2)], mg_send.at[e],
                mg_recv.at[e], to,
            )
        )
    for move in moves:
        move.start()

    row_id = lax.broadcasted_iota(jnp.int32, (pair_rows, pair_rows), 0)
    col_id = lax.broadcasted_iota(jnp.int32, (pair_rows, pair_rows), 1)
    reach = []
    place_col = []
    for p in range(pairs):
        above = parents[2 * p + 1 : 2 * p + 2, :]
        above = jnp.concatenate(
            [parents[2 * p : 2 * p + 1, :], jnp.where(above >= 0, above + draft, above)], axis=1
        )
        reach.append(((row_id == above) | (col_id == row_id)).astype(F32))
        level = jnp.concatenate(
            [depths[2 * p : 2 * p + 1, :], depths[2 * p + 1 : 2 * p + 2, :]], axis=1
        )
        depth_row[p] = level
        place_col.append(
            jnp.sum(
                jnp.where(row_id == col_id, level.astype(F32), 0.0), axis=1, keepdims=True
            )
        )
    for sweep in range(max(1, (draft - 1).bit_length())):
        for p in range(pairs):
            low = reach[p].astype(BF16)
            reach[p] = jnp.minimum(jnp.dot(low, low, preferred_element_type=F32), 1.0)
    for p in range(pairs):
        anc_tab[p] = reach[p].T

    for move in moves:
        move.wait()
    loads[4].wait()
    source = jnp.int32(0)
    for g in range(reps):
        source = jnp.where(migrate_to[g] == rep, g, source)
    came = moved_len[source][0:1, :]
    half_sign = jnp.where(
        lax.broadcasted_iota(jnp.int32, (1, head), 1) < head // 2, -1.0, 1.0
    ).astype(F32)
    for r in range(slots):
        is_new = (leaving == r).astype(jnp.int32)
        length = came * is_new + cache_len[r] * (1 - is_new)
        new_len[r] = length
        at = slice(r % 2 * draft, (r % 2 + 1) * draft)
        place = length.astype(F32) + place_col[r // 2][at]
        angle = place * freq[...]
        cos_tab[r * draft : (r + 1) * draft, :] = jnp.cos(angle)
        sin_tab[r * draft : (r + 1) * draft, :] = jnp.sin(angle) * half_sign
    hops = []
    if grid4:
        gathers[1].wait_send()
        gathers[2].start()
        gathers[1].wait_recv()
        held = block(rows, dst_chip(first) * 2 + core)
        hops.append(
            remote(
                held, held, ag_send.at[3], ag_recv.at[3],
                {"tp": dst_chip(second) * 2 + core},
            )
        )
        hops[0].start()
    for load in loads[:4]:
        load.wait()

    scale = 1.0 / math.sqrt(head)
    token = lax.broadcasted_iota(jnp.int32, (draft, 2 * pages.shape[1]), 1)
    forwards = []

    def arrive(d):
        if not grid4:
            gathers[d].wait_recv()
        elif d == 2:
            gathers[2].wait_recv()
        elif d == 3:
            hops[0].wait_recv()
        way = {1: first, 2: second, 3: 3}[d] if grid4 else d
        held = block(rows, src_chip(way) * 2 + core)
        forward = remote(held, held, fw_send.at[d], fw_recv.at[d], {"tp": sibling})
        forward.start()
        forwards.append(forward)

    def attend(p):
        first_row = pl.multiple_of(p * pair_rows, pair_rows)
        span = pl.ds(first_row, pair_rows)
        qkv = jnp.dot(rows[span, :], w_qkv[...], preferred_element_type=F32)
        cos = cos_tab[span, :]
        sin = sin_tab[span, :]
        q = qkv[:, :head]
        k = qkv[:, head : 2 * head]
        q = (q * cos + pltpu.roll(q, head // 2, 1) * sin).astype(BF16)
        k = (k * cos + pltpu.roll(k, head // 2, 1) * sin).astype(BF16)
        v = qkv[:, 2 * head :].astype(BF16)
        ancestry = anc_tab[p]
        nt = (((1,), (1,)), ((), ()))
        tree = lax.dot_general(q, k, nt, preferred_element_type=F32) * scale
        tree = jnp.where(ancestry > 0.5, tree, -1e30)
        attn = []
        for part in range(2):
            r = 2 * p + part
            at = slice(part * draft, (part + 1) * draft)
            is_new = (leaving == r).astype(jnp.int32)
            cache = jnp.concatenate(
                [
                    pages[
                        page_table[r, j] * (1 - is_new)
                        + (pool_pages + 2 * source + j) * is_new
                    ]
                    for j in range(2)
                ],
                axis=0,
            )
            cached = lax.dot_general(
                q[at], cache[:, :head], nt, preferred_element_type=F32
            ) * scale
            cached = jnp.where(token < new_len[r], cached, -1e30)
            peak = jnp.maximum(
                jnp.max(cached, axis=-1, keepdims=True),
                jnp.max(tree[at], axis=-1, keepdims=True),
            )
            p_cache = jnp.exp(cached - peak)
            p_tree = jnp.exp(tree[at] - peak)
            total = jnp.sum(p_cache, axis=-1, keepdims=True) + jnp.sum(
                p_tree, axis=-1, keepdims=True
            )
            summed = jnp.dot(
                p_cache.astype(BF16), cache[:, head:], preferred_element_type=F32
            ) + jnp.dot(p_tree.astype(BF16), v, preferred_element_type=F32)
            attn.append((summed / total).astype(BF16))
        attn = jnp.concatenate(attn, axis=0)

        tile = 512

        @pl.loop(0, width // tile)
        def _(i):
            c = pl.ds(pl.multiple_of(i * tile, tile), tile)
            terms[span, c] = lax.dot_general(
                attn, w_out[c, :], nt, preferred_element_type=F32
            ).astype(BF16)

        return (p, k, v, ancestry)

    def accept_path(state):
        p, k, v, ancestry = state
        node = row_id[:, :1]
        chosen = ((node == accept[2 * p]) | (node == accept[2 * p + 1] + draft)).astype(F32)
        on_path = jnp.sum(ancestry * chosen, axis=0, keepdims=True)
        level = depth_row[p] + jnp.where(col_id[:1] < draft, 0, draft)
        select = jnp.where(level == row_id, on_path, 0.0).astype(BF16)
        got_k = jnp.dot(select, k, preferred_element_type=F32).astype(BF16)
        got_v = jnp.dot(select, v, preferred_element_type=F32).astype(BF16)
        for part in range(2):
            at = slice(part * draft, (part + 1) * draft)
            accepted[2 * p + part, :, :head] = got_k[at]
            accepted[2 * p + part, :, head:] = got_v[at]

    swaps = {}

    def swap(d):
        c = src_chip(d)
        swaps[d] = remote(
            block(terms, c * 2 + 1 - core), pair_in.at[c], ps_send.at[d], ps_recv.at[d],
            {"tp": sibling},
        )
        swaps[d].start()

    sends = []

    def pair_and_send(d):
        c = src_chip(d)
        swaps[d].wait_recv()
        base = (c * 2 + core) * rows_dev

        @pl.loop(0, rows_dev // 16)
        def _(i):
            mine = terms[pl.ds(pl.multiple_of(base + i * 16, 16), 16), :].astype(F32)
            at = pl.ds(pl.multiple_of(i * 16, 16), 16)
            pair_sum[c, at, :] = (mine + pair_in[c, at, :].astype(F32)).astype(BF16)

        send = remote(
            pair_sum.at[c], rs_in.at[d], rs_send.at[d], rs_recv.at[d], {"tp": c * 2 + core}
        )
        send.start()
        sends.append(send)

    half = rows_dev // 2

    def add_up(c, start, count, relay):
        base = (c * 2 + core) * rows_dev

        @pl.loop(0, count // 16)
        def _(i):
            total = terms[
                pl.ds(pl.multiple_of(base + start + i * 16, 16), 16), :
            ].astype(F32)
            at = pl.ds(pl.multiple_of(start + i * 16, 16), 16)
            total = total + pair_in[c, at, :].astype(F32)
            if relay:
                total = total + rs_in[3, at, :].astype(F32)
            pair_sum[c, at, :] = total.astype(BF16)

    def post(c, slot, start, count, sem, way):
        at = pl.ds(start, count)
        sends.append(
            remote(
                pair_sum.at[c, at, :], rs_in.at[slot, at, :], rs_send.at[sem],
                rs_recv.at[sem], {"tp": dst_chip(way) * 2 + core},
            )
        )
        sends[-1].start()

    if grid4:
        near, far, across = dst_chip(first), dst_chip(second), dst_chip(3)
        arrive(1)
        gathers[0].wait_recv()
        state = attend(chip)
        swap(0)
        accept_path(state)
        arrive(2)
        for forward in forwards:
            forward.wait_recv()
        for d in (1, 2):
            state = attend(src_chip(d))
            swap(d)
            accept_path(state)
        arrive(3)
        for d in (1, 2):
            swaps[d].wait_recv()
        add_up(near, 0, rows_dev, False)
        post(near, 1, 0, rows_dev, 1, first)
        forwards[2].wait_recv()
        state = attend(across)
        swap(3)
        swaps[3].wait_recv()
        for part in range(2):
            add_up(across, part * half, half, False)
            post(across, 3, part * half, half, 3 + part, first)
        relays = sends[1:3]
        accept_path(state)
        for part in range(2):
            relays[part].wait_recv()
            add_up(far, part * half, half, True)
            post(far, 2, part * half, half, (2, 5)[part], second)
        last = [sends[0], sends[3], sends[4]]
    else:
        gathers[0].wait_recv()
        for d in range(1, chips):
            arrive(d)
        for forward in forwards:
            forward.wait_recv()
        for p in range(pairs):
            accept_path(attend(p))
        for d in range(chips):
            swap(d)
        for d in range(1, chips):
            pair_and_send(d)
        last = sends

    swaps[0].wait_recv()
    for send in last:
        send.wait_recv()

    @pl.loop(0, rows_dev // 16)
    def _(i):
        at = pl.ds(pl.multiple_of(i * 16, 16), 16)
        total = terms[pl.ds(pl.multiple_of(own + i * 16, 16), 16), :].astype(F32)
        total = total + pair_in[chip, at, :].astype(F32)
        for d in range(1, 3 if grid4 else chips):
            total = total + rs_in[d, at, :].astype(F32)
        out[at, :] = (hidden[at, :].astype(F32) + total).astype(BF16)

    done = gathers[1] if grid4 else None
    for copy in [g for g in gathers if g is not done] + hops + forwards + list(swaps.values()) + sends:
        copy.wait_send()


def local(
    n,
    reps,
    hidden,
    norm_gain,
    w_query,
    w_key,
    w_value,
    w_output,
    kv_pool,
    page_table,
    cache_len,
    parents,
    depths,
    accept_node,
    migrate_to,
    leave_slot,
):
    slots, draft = parents.shape
    rows_dev, width = hidden.shape
    head = w_query.shape[1]
    count = slots * draft
    chips = n // 2
    lane = jnp.arange(head, dtype=jnp.int32) % (head // 2)
    freq = (rope_base ** (-(lane.astype(F32) * 2.0 / head)))[None, :]
    vmem = pl.BlockSpec(memory_space=pltpu.VMEM)
    hbm = pl.BlockSpec(memory_space=pl.ANY)
    dma = pltpu.SemaphoreType.DMA
    page = kv_pool.shape[1]
    return pl.pallas_call(
        functools.partial(kernel, n, reps),
        out_shape=(
            jax.ShapeDtypeStruct((rows_dev, width), BF16),
            jax.ShapeDtypeStruct((slots, draft, 2 * head), BF16),
        ),
        in_specs=[vmem] * 6 + [hbm] * 9,
        out_specs=(vmem, vmem),
        scratch_shapes=[
            pltpu.VMEM((count, width), BF16),
            pltpu.VMEM((width, 3 * head), BF16),
            pltpu.VMEM((width, head), BF16),
            pltpu.VMEM((kv_pool.shape[0] + 2 * reps, page, 2 * head), BF16),
            pltpu.VMEM((reps, 8, head), jnp.int32),
            pltpu.VMEM((slots, 1, head), jnp.int32),
            pltpu.VMEM((count, head), F32),
            pltpu.VMEM((count, head), F32),
            pltpu.VMEM((slots // 2, 2 * draft, 2 * draft), F32),
            pltpu.SMEM(page_table.shape, jnp.int32),
            pltpu.SMEM(cache_len.shape, jnp.int32),
            pltpu.SMEM(accept_node.shape, jnp.int32),
            pltpu.SMEM(migrate_to.shape, jnp.int32),
            pltpu.SMEM(leave_slot.shape, jnp.int32),
            pltpu.VMEM((slots // 2, 1, 2 * draft), jnp.int32),
            pltpu.VMEM((count, width), BF16),
            pltpu.VMEM((chips, rows_dev, width), BF16),
            pltpu.VMEM((chips, rows_dev, width), BF16),
            pltpu.VMEM((chips, rows_dev, width), BF16),
            dma((10,)),
        ]
        + [dma((chips,))] * 6
        + [dma((chips + 2,))] * 2
        + [dma((reps,))] * 4,
        compiler_params=pltpu.CompilerParams(
            collective_id=0, has_side_effects=True, vmem_limit_bytes=48 * 1024 * 1024
        ),
    )(
        hidden,
        norm_gain[None, :],
        kv_pool,
        parents,
        depths,
        freq,
        page_table,
        cache_len,
        accept_node,
        migrate_to,
        leave_slot,
        w_query,
        w_key,
        w_value,
        w_output,
    )


def solution(mesh):
    in_specs = (
        P(("rep", "tp"), None),
        P(),
        P(None, "tp"),
        P(None, "tp"),
        P(None, "tp"),
        P(None, "tp"),
        P("rep", None, "tp"),
        P("rep", None),
        P("rep"),
        P("rep", None),
        P("rep", None),
        P("rep"),
        P(),
        P(),
    )
    out_specs = (P(("rep", "tp"), None), P("rep", None, "tp"))
    fn = functools.partial(local, mesh.shape["tp"], mesh.shape["rep"])
    return jax.shard_map(fn, mesh=mesh, in_specs=in_specs, out_specs=out_specs, check_vma=False)
```

```python
import functools
import math

import jax
import jax.numpy as jnp
from jax import lax
from jax.experimental import pallas as pl
from jax.experimental.pallas import tpu as pltpu
from jax.sharding import PartitionSpec as P

eps = 1e-05
rope_base = 1000000.0
MESH = pl.DeviceIdType.MESH
F32 = jnp.float32
BF16 = jnp.bfloat16


def kernel(
    n,
    reps,
    gain,
    parents,
    depths,
    freq,
    hidden_in,
    pool_in,
    page_table_in,
    cache_len_in,
    accept_in,
    migrate_to_in,
    leave_slot_in,
    w_query,
    w_key,
    w_value,
    w_output,
    out,
    accepted,
    rows,
    w_qkv,
    w_out,
    pages,
    moved_len,
    new_len,
    cos_tab,
    sin_tab,
    anc_tab,
    page_table,
    cache_len,
    accept,
    migrate_to,
    leave_slot,
    depth_row,
    hidden,
    pool,
    w_out_t,
    terms,
    pair_in,
    pair_sum,
    rs_in,
    local_sem,
    ag_send,
    ag_recv,
    fw_send,
    fw_recv,
    ps_send,
    ps_recv,
    rs_send,
    rs_recv,
    mg_send,
    mg_recv,
    ml_send,
    ml_recv,
):
    chips = n // 2
    rows_dev, width = hidden.shape
    head = w_out.shape[1]
    slots = parents.shape[0]
    draft = rows.shape[0] // slots
    pair_rows = 2 * draft
    pairs = slots // 2
    pool_pages = pool.shape[0]
    rep = lax.axis_index("rep")
    me = lax.axis_index("tp")
    core = me % 2
    chip = me // 2
    sibling = chip * 2 + (1 - core)
    grid4 = chips == 4 and slots == 2 * chips
    first = 1 + core
    second = 2 - core

    def dst_chip(d):
        if chips == 4:
            return ((chip // 2 + d // 2) % 2) * 2 + (chip % 2 + d % 2) % 2
        return (chip + d) % chips

    def src_chip(d):
        if chips == 4:
            return dst_chip(d)
        return (chip + chips - d) % chips

    def block(ref, dev):
        return ref.at[pl.ds(pl.multiple_of(dev * rows_dev, rows_dev), rows_dev), :]

    def remote(src, dst, send, recv, where):
        return pltpu.make_async_remote_copy(
            src_ref=src, dst_ref=dst, send_sem=send, recv_sem=recv,
            device_id=where, device_id_type=MESH,
        )

    loads = [
        pltpu.make_async_copy(w_query, w_qkv.at[:, pl.ds(0, head)], local_sem.at[0]),
        pltpu.make_async_copy(w_key, w_qkv.at[:, pl.ds(head, head)], local_sem.at[1]),
        pltpu.make_async_copy(w_value, w_qkv.at[:, pl.ds(2 * head, head)], local_sem.at[2]),
        pltpu.make_async_copy(w_output, w_out, local_sem.at[3]),
        pltpu.make_async_copy(pool_in, pages.at[pl.ds(0, pool_pages)], local_sem.at[4]),
    ]
    small = [
        pltpu.make_async_copy(pool_in, pool, local_sem.at[10]),
        pltpu.make_async_copy(page_table_in, page_table, local_sem.at[5]),
        pltpu.make_async_copy(cache_len_in, cache_len, local_sem.at[6]),
        pltpu.make_async_copy(accept_in, accept, local_sem.at[7]),
        pltpu.make_async_copy(migrate_to_in, migrate_to, local_sem.at[8]),
        pltpu.make_async_copy(leave_slot_in, leave_slot, local_sem.at[9]),
    ]
    barrier = pltpu.get_barrier_semaphore()
    pl.semaphore_signal(barrier, inc=1, device_id={"tp": sibling}, device_id_type=MESH)
    for d in range(1, chips):
        pl.semaphore_signal(
            barrier, inc=1, device_id={"tp": dst_chip(d) * 2 + core}, device_id_type=MESH
        )
    for e in range(1, reps):
        pl.semaphore_signal(
            barrier, inc=1, device_id={"rep": (rep + e) % reps}, device_id_type=MESH
        )
    load_hidden = pltpu.make_async_copy(hidden_in, hidden, local_sem.at[11])
    for load in [load_hidden] + small + loads:
        load.start()
    load_hidden.wait()

    own = pl.multiple_of(me * rows_dev, rows_dev)

    @pl.loop(0, rows_dev // 16)
    def _(i):
        x = hidden[pl.ds(pl.multiple_of(i * 16, 16), 16), :].astype(F32)
        mean = jnp.mean(x * x, axis=-1, keepdims=True)
        y = x * lax.rsqrt(mean + eps) * gain[...].astype(F32)
        rows[pl.ds(pl.multiple_of(own + i * 16, 16), 16), :] = y.astype(BF16)

    for load in small:
        load.wait()
    leaving = leave_slot[rep]
    tail = pool_pages + 2 * rep
    pages[tail] = pool[page_table[leaving, 0]]
    pages[tail + 1] = pool[page_table[leaving, 1]]
    moved_len[rep] = jnp.full(moved_len.shape[1:], cache_len[leaving], jnp.int32)

    pl.semaphore_wait(barrier, 1 + (chips - 1) + (reps - 1))

    gathers = [
        remote(block(rows, me), block(rows, me), ag_send.at[0], ag_recv.at[0], {"tp": sibling})
    ]
    for d in range(1, 3 if grid4 else chips):
        way = (first if d == 1 else second) if grid4 else d
        gathers.append(
            remote(
                block(rows, me), block(rows, me), ag_send.at[d], ag_recv.at[d],
                {"tp": dst_chip(way) * 2 + core},
            )
        )
    for d in [1, 0] if grid4 else list(range(1, chips)) + [0]:
        gathers[d].start()
    moves = []
    for e in range(1, reps):
        to = {"rep": (rep + e) % reps}
        moves.append(
            remote(moved_len.at[rep], moved_len.at[rep], ml_send.at[e], ml_recv.at[e], to)
        )
        moves.append(
            remote(
                pages.at[pl.ds(tail, 2)], pages.at[pl.ds(tail, 2)], mg_send.at[e],
                mg_recv.at[e], to,
            )
        )
    for move in moves:
        move.start()

    row_id = lax.broadcasted_iota(jnp.int32, (pair_rows, pair_rows), 0)
    col_id = lax.broadcasted_iota(jnp.int32, (pair_rows, pair_rows), 1)
    reach = []
    place_col = []
    for p in range(pairs):
        above = parents[2 * p + 1 : 2 * p + 2, :]
        above = jnp.concatenate(
            [parents[2 * p : 2 * p + 1, :], jnp.where(above >= 0, above + draft, above)], axis=1
        )
        reach.append(((row_id == above) | (col_id == row_id)).astype(F32))
        level = jnp.concatenate(
            [depths[2 * p : 2 * p + 1, :], depths[2 * p + 1 : 2 * p + 2, :]], axis=1
        )
        depth_row[p] = level
        place_col.append(
            jnp.sum(
                jnp.where(row_id == col_id, level.astype(F32), 0.0), axis=1, keepdims=True
            )
        )
    for sweep in range(max(1, (draft - 1).bit_length())):
        for p in range(pairs):
            low = reach[p].astype(BF16)
            reach[p] = jnp.minimum(jnp.dot(low, low, preferred_element_type=F32), 1.0)
    for p in range(pairs):
        anc_tab[p] = reach[p].T

    for move in moves:
        move.wait()
    loads[4].wait()
    source = jnp.int32(0)
    for g in range(reps):
        source = jnp.where(migrate_to[g] == rep, g, source)
    came = moved_len[source][0:1, :]
    half_sign = jnp.where(
        lax.broadcasted_iota(jnp.int32, (1, head), 1) < head // 2, -1.0, 1.0
    ).astype(F32)
    for r in range(slots):
        is_new = (leaving == r).astype(jnp.int32)
        length = came * is_new + cache_len[r] * (1 - is_new)
        new_len[r] = length
        at = slice(r % 2 * draft, (r % 2 + 1) * draft)
        place = length.astype(F32) + place_col[r // 2][at]
        angle = place * freq[...]
        cos_tab[r * draft : (r + 1) * draft, :] = jnp.cos(angle)
        sin_tab[r * draft : (r + 1) * draft, :] = jnp.sin(angle) * half_sign
    hops = []
    tile = 512
    loads[3].wait()
    if grid4:
        gathers[1].wait_send()
        gathers[2].start()

    @pl.loop(0, width // tile)
    def _(i):
        c = pl.ds(pl.multiple_of(i * tile, tile), tile)
        w_out_t[:, c] = w_out[c, :].T

    if grid4:
        gathers[1].wait_recv()
        held = block(rows, dst_chip(first) * 2 + core)
        hops.append(
            remote(
                held, held, ag_send.at[3], ag_recv.at[3],
                {"tp": dst_chip(second) * 2 + core},
            )
        )
        hops[0].start()
    for load in loads[:3]:
        load.wait()

    scale = 1.0 / math.sqrt(head)
    token = lax.broadcasted_iota(jnp.int32, (draft, 2 * pages.shape[1]), 1)
    forwards = []

    def arrive(d):
        if not grid4:
            gathers[d].wait_recv()
        elif d == 2:
            gathers[2].wait_recv()
        elif d == 3:
            hops[0].wait_recv()
        way = {1: first, 2: second, 3: 3}[d] if grid4 else d
        held = block(rows, src_chip(way) * 2 + core)
        forward = remote(held, held, fw_send.at[d], fw_recv.at[d], {"tp": sibling})
        forward.start()
        forwards.append(forward)

    def attend(p):
        first_row = pl.multiple_of(p * pair_rows, pair_rows)
        span = pl.ds(first_row, pair_rows)
        qkv = jnp.dot(rows[span, :], w_qkv[...], preferred_element_type=F32)
        cos = cos_tab[span, :]
        sin = sin_tab[span, :]
        q = qkv[:, :head]
        k = qkv[:, head : 2 * head]
        q = (q * cos + pltpu.roll(q, head // 2, 1) * sin).astype(BF16)
        k = (k * cos + pltpu.roll(k, head // 2, 1) * sin).astype(BF16)
        v = qkv[:, 2 * head :].astype(BF16)
        ancestry = anc_tab[p]
        nt = (((1,), (1,)), ((), ()))
        tree = lax.dot_general(q, k, nt, preferred_element_type=F32) * scale
        tree = jnp.where(ancestry > 0.5, tree, -1e30)
        attn = []
        for part in range(2):
            r = 2 * p + part
            at = slice(part * draft, (part + 1) * draft)
            is_new = (leaving == r).astype(jnp.int32)
            cache = jnp.concatenate(
                [
                    pages[
                        page_table[r, j] * (1 - is_new)
                        + (pool_pages + 2 * source + j) * is_new
                    ]
                    for j in range(2)
                ],
                axis=0,
            )
            cached = lax.dot_general(
                q[at], cache[:, :head], nt, preferred_element_type=F32
            ) * scale
            cached = jnp.where(token < new_len[r], cached, -1e30)
            peak = jnp.maximum(
                jnp.max(cached, axis=-1, keepdims=True),
                jnp.max(tree[at], axis=-1, keepdims=True),
            )
            p_cache = jnp.exp(cached - peak)
            p_tree = jnp.exp(tree[at] - peak)
            total = jnp.sum(p_cache, axis=-1, keepdims=True) + jnp.sum(
                p_tree, axis=-1, keepdims=True
            )
            summed = jnp.dot(
                p_cache.astype(BF16), cache[:, head:], preferred_element_type=F32
            ) + jnp.dot(p_tree.astype(BF16), v, preferred_element_type=F32)
            attn.append((summed / total).astype(BF16))
        attn = jnp.concatenate(attn, axis=0)

        @pl.loop(0, width // tile)
        def _(i):
            c = pl.ds(pl.multiple_of(i * tile, tile), tile)
            terms[span, c] = jnp.dot(
                attn, w_out_t[:, c], preferred_element_type=F32
            ).astype(BF16)

        return (p, k, v, ancestry)

    def accept_path(state):
        p, k, v, ancestry = state
        node = row_id[:, :1]
        chosen = ((node == accept[2 * p]) | (node == accept[2 * p + 1] + draft)).astype(F32)
        on_path = jnp.sum(ancestry * chosen, axis=0, keepdims=True)
        level = depth_row[p] + jnp.where(col_id[:1] < draft, 0, draft)
        select = jnp.where(level == row_id, on_path, 0.0).astype(BF16)
        got_k = jnp.dot(select, k, preferred_element_type=F32).astype(BF16)
        got_v = jnp.dot(select, v, preferred_element_type=F32).astype(BF16)
        for part in range(2):
            at = slice(part * draft, (part + 1) * draft)
            accepted[2 * p + part, :, :head] = got_k[at]
            accepted[2 * p + part, :, head:] = got_v[at]

    swaps = {}

    def swap(d):
        c = src_chip(d)
        swaps[d] = remote(
            block(terms, c * 2 + 1 - core), pair_in.at[c], ps_send.at[d], ps_recv.at[d],
            {"tp": sibling},
        )
        swaps[d].start()

    sends = []

    def pair_and_send(d):
        c = src_chip(d)
        swaps[d].wait_recv()
        base = (c * 2 + core) * rows_dev

        @pl.loop(0, rows_dev // 16)
        def _(i):
            mine = terms[pl.ds(pl.multiple_of(base + i * 16, 16), 16), :].astype(F32)
            at = pl.ds(pl.multiple_of(i * 16, 16), 16)
            pair_sum[c, at, :] = (mine + pair_in[c, at, :].astype(F32)).astype(BF16)

        send = remote(
            pair_sum.at[c], rs_in.at[d], rs_send.at[d], rs_recv.at[d], {"tp": c * 2 + core}
        )
        send.start()
        sends.append(send)

    half = rows_dev // 2

    def add_up(c, start, count, relay):
        base = (c * 2 + core) * rows_dev

        @pl.loop(0, count // 16)
        def _(i):
            total = terms[
                pl.ds(pl.multiple_of(base + start + i * 16, 16), 16), :
            ].astype(F32)
            at = pl.ds(pl.multiple_of(start + i * 16, 16), 16)
            total = total + pair_in[c, at, :].astype(F32)
            if relay:
                total = total + rs_in[3, at, :].astype(F32)
            pair_sum[c, at, :] = total.astype(BF16)

    def post(c, slot, start, count, sem, way):
        at = pl.ds(start, count)
        sends.append(
            remote(
                pair_sum.at[c, at, :], rs_in.at[slot, at, :], rs_send.at[sem],
                rs_recv.at[sem], {"tp": dst_chip(way) * 2 + core},
            )
        )
        sends[-1].start()

    if grid4:
        near, far, across = dst_chip(first), dst_chip(second), dst_chip(3)
        arrive(1)
        gathers[0].wait_recv()
        state = attend(chip)
        swap(0)
        accept_path(state)
        arrive(2)
        for forward in forwards:
            forward.wait_recv()
        for d in (1, 2):
            state = attend(src_chip(d))
            swap(d)
            accept_path(state)
        arrive(3)
        for d in (1, 2):
            swaps[d].wait_recv()
        add_up(near, 0, rows_dev, False)
        post(near, 1, 0, rows_dev, 1, first)
        forwards[2].wait_recv()
        state = attend(across)
        swap(3)
        swaps[3].wait_recv()
        for part in range(2):
            add_up(across, part * half, half, False)
            post(across, 3, part * half, half, 3 + part, first)
        relays = sends[1:3]
        accept_path(state)
        for part in range(2):
            relays[part].wait_recv()
            add_up(far, part * half, half, True)
            post(far, 2, part * half, half, (2, 5)[part], second)
        last = [sends[0], sends[3], sends[4]]
    else:
        gathers[0].wait_recv()
        for d in range(1, chips):
            arrive(d)
        for forward in forwards:
            forward.wait_recv()
        for p in range(pairs):
            accept_path(attend(p))
        for d in range(chips):
            swap(d)
        for d in range(1, chips):
            pair_and_send(d)
        last = sends

    swaps[0].wait_recv()
    for send in last:
        send.wait_recv()

    @pl.loop(0, rows_dev // 16)
    def _(i):
        at = pl.ds(pl.multiple_of(i * 16, 16), 16)
        total = terms[pl.ds(pl.multiple_of(own + i * 16, 16), 16), :].astype(F32)
        total = total + pair_in[chip, at, :].astype(F32)
        for d in range(1, 3 if grid4 else chips):
            total = total + rs_in[d, at, :].astype(F32)
        out[at, :] = (hidden[at, :].astype(F32) + total).astype(BF16)

    done = gathers[1] if grid4 else None
    for copy in [g for g in gathers if g is not done] + hops + forwards + list(swaps.values()) + sends:
        copy.wait_send()


def local(
    n,
    reps,
    hidden,
    norm_gain,
    w_query,
    w_key,
    w_value,
    w_output,
    kv_pool,
    page_table,
    cache_len,
    parents,
    depths,
    accept_node,
    migrate_to,
    leave_slot,
):
    slots, draft = parents.shape
    rows_dev, width = hidden.shape
    head = w_query.shape[1]
    count = slots * draft
    chips = n // 2
    lane = jnp.arange(head, dtype=jnp.int32) % (head // 2)
    freq = (rope_base ** (-(lane.astype(F32) * 2.0 / head)))[None, :]
    vmem = pl.BlockSpec(memory_space=pltpu.VMEM)
    hbm = pl.BlockSpec(memory_space=pltpu.HBM)
    dma = pltpu.SemaphoreType.DMA
    page = kv_pool.shape[1]
    return pl.pallas_call(
        functools.partial(kernel, n, reps),
        out_shape=(
            jax.ShapeDtypeStruct((rows_dev, width), BF16),
            jax.ShapeDtypeStruct((slots, draft, 2 * head), BF16),
        ),
        in_specs=[vmem] * 4 + [hbm] * 2 + [pl.BlockSpec(memory_space=pl.ANY)] * 5 + [hbm] * 4,
        out_specs=(vmem, vmem),
        scratch_shapes=[
            pltpu.VMEM((count, width), BF16),
            pltpu.VMEM((width, 3 * head), BF16),
            pltpu.VMEM((width, head), BF16),
            pltpu.VMEM((kv_pool.shape[0] + 2 * reps, page, 2 * head), BF16),
            pltpu.VMEM((reps, 8, head), jnp.int32),
            pltpu.VMEM((slots, 1, head), jnp.int32),
            pltpu.VMEM((count, head), F32),
            pltpu.VMEM((count, head), F32),
            pltpu.VMEM((slots // 2, 2 * draft, 2 * draft), F32),
            pltpu.SMEM(page_table.shape, jnp.int32),
            pltpu.SMEM(cache_len.shape, jnp.int32),
            pltpu.SMEM(accept_node.shape, jnp.int32),
            pltpu.SMEM(migrate_to.shape, jnp.int32),
            pltpu.SMEM(leave_slot.shape, jnp.int32),
            pltpu.VMEM((slots // 2, 1, 2 * draft), jnp.int32),
            pltpu.VMEM((rows_dev, width), BF16),
            pltpu.VMEM(kv_pool.shape, BF16),
            pltpu.VMEM((head, width), BF16),
            pltpu.VMEM((count, width), BF16),
            pltpu.VMEM((chips, rows_dev, width), BF16),
            pltpu.VMEM((chips, rows_dev, width), BF16),
            pltpu.VMEM((chips, rows_dev, width), BF16),
            dma((12,)),
        ]
        + [dma((chips,))] * 6
        + [dma((chips + 2,))] * 2
        + [dma((reps,))] * 4,
        compiler_params=pltpu.CompilerParams(
            collective_id=0, has_side_effects=True, vmem_limit_bytes=60 * 1024 * 1024
        ),
    )(
        norm_gain[None, :],
        parents,
        depths,
        freq,
        hidden,
        kv_pool,
        page_table,
        cache_len,
        accept_node,
        migrate_to,
        leave_slot,
        w_query,
        w_key,
        w_value,
        w_output,
    )


def solution(mesh):
    in_specs = (
        P(("rep", "tp"), None),
        P(),
        P(None, "tp"),
        P(None, "tp"),
        P(None, "tp"),
        P(None, "tp"),
        P("rep", None, "tp"),
        P("rep", None),
        P("rep"),
        P("rep", None),
        P("rep", None),
        P("rep"),
        P(),
        P(),
    )
    out_specs = (P(("rep", "tp"), None), P("rep", None, "tp"))
    fn = functools.partial(local, mesh.shape["tp"], mesh.shape["rep"])
    return jax.shard_map(fn, mesh=mesh, in_specs=in_specs, out_specs=out_specs, check_vma=False)
```

```python
import functools
import math

import jax
import jax.numpy as jnp
from jax import lax
from jax.experimental import pallas as pl
from jax.experimental.pallas import tpu as pltpu
from jax.sharding import PartitionSpec as P

eps = 1e-05
rope_base = 1000000.0
MESH = pl.DeviceIdType.MESH
F32 = jnp.float32
BF16 = jnp.bfloat16


def kernel(
    n,
    reps,
    gain,
    parents,
    depths,
    hidden_in,
    pool_in,
    page_table_in,
    cache_len_in,
    accept_in,
    migrate_to_in,
    leave_slot_in,
    w_query,
    w_key,
    w_value,
    w_output,
    out,
    accepted,
    rows,
    w_qkv,
    w_out,
    pages,
    moved_len,
    new_len,
    cos_tab,
    sin_tab,
    anc_tab,
    page_table,
    cache_len,
    accept,
    migrate_to,
    leave_slot,
    depth_row,
    hidden,
    pool,
    w_out_t,
    terms,
    pair_in,
    pair_sum,
    rs_in,
    local_sem,
    ag_send,
    ag_recv,
    fw_send,
    fw_recv,
    ps_send,
    ps_recv,
    rs_send,
    rs_recv,
    mg_send,
    mg_recv,
    ml_send,
    ml_recv,
):
    chips = n // 2
    rows_dev, width = hidden.shape
    head = w_out.shape[1]
    slots = parents.shape[0]
    draft = rows.shape[0] // slots
    pair_rows = 2 * draft
    pairs = slots // 2
    pool_pages = pool.shape[0]
    rep = lax.axis_index("rep")
    me = lax.axis_index("tp")
    core = me % 2
    chip = me // 2
    sibling = chip * 2 + (1 - core)
    grid4 = chips == 4 and slots == 2 * chips
    first = 1 + core
    second = 2 - core

    def dst_chip(d):
        if chips == 4:
            return ((chip // 2 + d // 2) % 2) * 2 + (chip % 2 + d % 2) % 2
        return (chip + d) % chips

    def src_chip(d):
        if chips == 4:
            return dst_chip(d)
        return (chip + chips - d) % chips

    def block(ref, dev):
        return ref.at[pl.ds(pl.multiple_of(dev * rows_dev, rows_dev), rows_dev), :]

    def remote(src, dst, send, recv, where):
        return pltpu.make_async_remote_copy(
            src_ref=src, dst_ref=dst, send_sem=send, recv_sem=recv,
            device_id=where, device_id_type=MESH,
        )

    loads = [
        pltpu.make_async_copy(w_query, w_qkv.at[:, pl.ds(0, head)], local_sem.at[0]),
        pltpu.make_async_copy(w_key, w_qkv.at[:, pl.ds(head, head)], local_sem.at[1]),
        pltpu.make_async_copy(w_value, w_qkv.at[:, pl.ds(2 * head, head)], local_sem.at[2]),
        pltpu.make_async_copy(w_output, w_out, local_sem.at[3]),
        pltpu.make_async_copy(pool_in, pages.at[pl.ds(0, pool_pages)], local_sem.at[4]),
    ]
    small = [
        pltpu.make_async_copy(pool_in, pool, local_sem.at[10]),
        pltpu.make_async_copy(page_table_in, page_table, local_sem.at[5]),
        pltpu.make_async_copy(cache_len_in, cache_len, local_sem.at[6]),
        pltpu.make_async_copy(accept_in, accept, local_sem.at[7]),
        pltpu.make_async_copy(migrate_to_in, migrate_to, local_sem.at[8]),
        pltpu.make_async_copy(leave_slot_in, leave_slot, local_sem.at[9]),
    ]
    barrier = pltpu.get_barrier_semaphore()
    pl.semaphore_signal(barrier, inc=1, device_id={"tp": sibling}, device_id_type=MESH)
    for d in range(1, chips):
        pl.semaphore_signal(
            barrier, inc=1, device_id={"tp": dst_chip(d) * 2 + core}, device_id_type=MESH
        )
    for e in range(1, reps):
        pl.semaphore_signal(
            barrier, inc=1, device_id={"rep": (rep + e) % reps}, device_id_type=MESH
        )
    load_hidden = pltpu.make_async_copy(hidden_in, hidden, local_sem.at[11])
    for load in [load_hidden] + small + loads:
        load.start()
    load_hidden.wait()

    gain_row = gain[...].astype(F32).reshape(1, width)
    own = pl.multiple_of(me * rows_dev, rows_dev)

    @pl.loop(0, rows_dev // 16)
    def _(i):
        x = hidden[pl.ds(pl.multiple_of(i * 16, 16), 16), :].astype(F32)
        mean = jnp.mean(x * x, axis=-1, keepdims=True)
        y = x * lax.rsqrt(mean + eps) * gain_row
        rows[pl.ds(pl.multiple_of(own + i * 16, 16), 16), :] = y.astype(BF16)

    for load in small:
        load.wait()
    leaving = leave_slot[rep]
    tail = pool_pages + 2 * rep
    pages[tail] = pool[page_table[leaving, 0]]
    pages[tail + 1] = pool[page_table[leaving, 1]]
    moved_len[rep] = jnp.full(moved_len.shape[1:], cache_len[leaving], jnp.int32)

    pl.semaphore_wait(barrier, 1 + (chips - 1) + (reps - 1))

    gathers = [
        remote(block(rows, me), block(rows, me), ag_send.at[0], ag_recv.at[0], {"tp": sibling})
    ]
    for d in range(1, 3 if grid4 else chips):
        way = (first if d == 1 else second) if grid4 else d
        gathers.append(
            remote(
                block(rows, me), block(rows, me), ag_send.at[d], ag_recv.at[d],
                {"tp": dst_chip(way) * 2 + core},
            )
        )
    for d in [1, 0] if grid4 else list(range(1, chips)) + [0]:
        gathers[d].start()
    moves = []
    for e in range(1, reps):
        to = {"rep": (rep + e) % reps}
        moves.append(
            remote(moved_len.at[rep], moved_len.at[rep], ml_send.at[e], ml_recv.at[e], to)
        )
        moves.append(
            remote(
                pages.at[pl.ds(tail, 2)], pages.at[pl.ds(tail, 2)], mg_send.at[e],
                mg_recv.at[e], to,
            )
        )
    for move in moves:
        move.start()

    row_id = lax.broadcasted_iota(jnp.int32, (pair_rows, pair_rows), 0)
    col_id = lax.broadcasted_iota(jnp.int32, (pair_rows, pair_rows), 1)
    reach = []
    place_col = []
    for p in range(pairs):
        above = parents[2 * p + 1 : 2 * p + 2, :]
        above = jnp.concatenate(
            [parents[2 * p : 2 * p + 1, :], jnp.where(above >= 0, above + draft, above)], axis=1
        )
        reach.append(((row_id == above) | (col_id == row_id)).astype(F32))
        level = jnp.concatenate(
            [depths[2 * p : 2 * p + 1, :], depths[2 * p + 1 : 2 * p + 2, :]], axis=1
        )
        depth_row[p] = level
        place_col.append(
            jnp.sum(
                jnp.where(row_id == col_id, level.astype(F32), 0.0), axis=1, keepdims=True
            )
        )
    for sweep in range(max(1, (draft - 1).bit_length())):
        for p in range(pairs):
            low = reach[p].astype(BF16)
            reach[p] = jnp.minimum(jnp.dot(low, low, preferred_element_type=F32), 1.0)
    for p in range(pairs):
        anc_tab[p] = reach[p].T

    for move in moves:
        move.wait()
    loads[4].wait()
    source = jnp.int32(0)
    for g in range(reps):
        source = jnp.where(migrate_to[g] == rep, g, source)
    lane = lax.broadcasted_iota(jnp.int32, (1, head), 1) % (head // 2)
    freq = jnp.exp(lane.astype(F32) * (-2.0 / head * math.log(rope_base)))
    came = moved_len[source][0:1, :]
    half_sign = jnp.where(
        lax.broadcasted_iota(jnp.int32, (1, head), 1) < head // 2, -1.0, 1.0
    ).astype(F32)
    for r in range(slots):
        is_new = (leaving == r).astype(jnp.int32)
        length = came * is_new + cache_len[r] * (1 - is_new)
        new_len[r] = length
        at = slice(r % 2 * draft, (r % 2 + 1) * draft)
        place = length.astype(F32) + place_col[r // 2][at]
        angle = place * freq
        cos_tab[r * draft : (r + 1) * draft, :] = jnp.cos(angle)
        sin_tab[r * draft : (r + 1) * draft, :] = jnp.sin(angle) * half_sign
    hops = []
    tile = 512
    loads[3].wait()
    if grid4:
        gathers[1].wait_send()
        gathers[2].start()

    @pl.loop(0, width // tile)
    def _(i):
        c = pl.ds(pl.multiple_of(i * tile, tile), tile)
        w_out_t[:, c] = w_out[c, :].T

    if grid4:
        gathers[1].wait_recv()
        held = block(rows, dst_chip(first) * 2 + core)
        hops.append(
            remote(
                held, held, ag_send.at[3], ag_recv.at[3],
                {"tp": dst_chip(second) * 2 + core},
            )
        )
        hops[0].start()
    for load in loads[:3]:
        load.wait()

    scale = 1.0 / math.sqrt(head)
    token = lax.broadcasted_iota(jnp.int32, (draft, 2 * pages.shape[1]), 1)
    forwards = []

    def arrive(d):
        if not grid4:
            gathers[d].wait_recv()
        elif d == 2:
            gathers[2].wait_recv()
        elif d == 3:
            hops[0].wait_recv()
        way = {1: first, 2: second, 3: 3}[d] if grid4 else d
        held = block(rows, src_chip(way) * 2 + core)
        forward = remote(held, held, fw_send.at[d], fw_recv.at[d], {"tp": sibling})
        forward.start()
        forwards.append(forward)

    def attend(p):
        first_row = pl.multiple_of(p * pair_rows, pair_rows)
        span = pl.ds(first_row, pair_rows)
        qkv = jnp.dot(rows[span, :], w_qkv[...], preferred_element_type=F32)
        cos = cos_tab[span, :]
        sin = sin_tab[span, :]
        q = qkv[:, :head]
        k = qkv[:, head : 2 * head]
        q = (q * cos + pltpu.roll(q, head // 2, 1) * sin).astype(BF16)
        k = (k * cos + pltpu.roll(k, head // 2, 1) * sin).astype(BF16)
        v = qkv[:, 2 * head :].astype(BF16)
        ancestry = anc_tab[p]
        nt = (((1,), (1,)), ((), ()))
        tree = lax.dot_general(q, k, nt, preferred_element_type=F32) * scale
        tree = jnp.where(ancestry > 0.5, tree, -1e30)
        attn = []
        for part in range(2):
            r = 2 * p + part
            at = slice(part * draft, (part + 1) * draft)
            is_new = (leaving == r).astype(jnp.int32)
            cache = jnp.concatenate(
                [
                    pages[
                        page_table[r, j] * (1 - is_new)
                        + (pool_pages + 2 * source + j) * is_new
                    ]
                    for j in range(2)
                ],
                axis=0,
            )
            cached = lax.dot_general(
                q[at], cache[:, :head], nt, preferred_element_type=F32
            ) * scale
            cached = jnp.where(token < new_len[r], cached, -1e30)
            peak = jnp.maximum(
                jnp.max(cached, axis=-1, keepdims=True),
                jnp.max(tree[at], axis=-1, keepdims=True),
            )
            p_cache = jnp.exp(cached - peak)
            p_tree = jnp.exp(tree[at] - peak)
            total = jnp.sum(p_cache, axis=-1, keepdims=True) + jnp.sum(
                p_tree, axis=-1, keepdims=True
            )
            summed = jnp.dot(
                p_cache.astype(BF16), cache[:, head:], preferred_element_type=F32
            ) + jnp.dot(p_tree.astype(BF16), v, preferred_element_type=F32)
            attn.append((summed / total).astype(BF16))
        attn = jnp.concatenate(attn, axis=0)

        @pl.loop(0, width // tile)
        def _(i):
            c = pl.ds(pl.multiple_of(i * tile, tile), tile)
            terms[span, c] = jnp.dot(
                attn, w_out_t[:, c], preferred_element_type=F32
            ).astype(BF16)

        return (p, k, v, ancestry)

    def accept_path(state):
        p, k, v, ancestry = state
        node = row_id[:, :1]
        chosen = ((node == accept[2 * p]) | (node == accept[2 * p + 1] + draft)).astype(F32)
        on_path = jnp.sum(ancestry * chosen, axis=0, keepdims=True)
        level = depth_row[p] + jnp.where(col_id[:1] < draft, 0, draft)
        select = jnp.where(level == row_id, on_path, 0.0).astype(BF16)
        got_k = jnp.dot(select, k, preferred_element_type=F32).astype(BF16)
        got_v = jnp.dot(select, v, preferred_element_type=F32).astype(BF16)
        for part in range(2):
            at = slice(part * draft, (part + 1) * draft)
            accepted[2 * p + part, :, :head] = got_k[at]
            accepted[2 * p + part, :, head:] = got_v[at]

    swaps = {}

    def swap(d):
        c = src_chip(d)
        swaps[d] = remote(
            block(terms, c * 2 + 1 - core), pair_in.at[c], ps_send.at[d], ps_recv.at[d],
            {"tp": sibling},
        )
        swaps[d].start()

    sends = []

    def pair_and_send(d):
        c = src_chip(d)
        swaps[d].wait_recv()
        base = (c * 2 + core) * rows_dev

        @pl.loop(0, rows_dev // 16)
        def _(i):
            mine = terms[pl.ds(pl.multiple_of(base + i * 16, 16), 16), :].astype(F32)
            at = pl.ds(pl.multiple_of(i * 16, 16), 16)
            pair_sum[c, at, :] = (mine + pair_in[c, at, :].astype(F32)).astype(BF16)

        send = remote(
            pair_sum.at[c], rs_in.at[d], rs_send.at[d], rs_recv.at[d], {"tp": c * 2 + core}
        )
        send.start()
        sends.append(send)

    half = rows_dev // 2

    def add_up(c, start, count, relay):
        base = (c * 2 + core) * rows_dev

        @pl.loop(0, count // 16)
        def _(i):
            total = terms[
                pl.ds(pl.multiple_of(base + start + i * 16, 16), 16), :
            ].astype(F32)
            at = pl.ds(pl.multiple_of(start + i * 16, 16), 16)
            total = total + pair_in[c, at, :].astype(F32)
            if relay:
                total = total + rs_in[3, at, :].astype(F32)
            pair_sum[c, at, :] = total.astype(BF16)

    def post(c, slot, start, count, sem, way):
        at = pl.ds(start, count)
        sends.append(
            remote(
                pair_sum.at[c, at, :], rs_in.at[slot, at, :], rs_send.at[sem],
                rs_recv.at[sem], {"tp": dst_chip(way) * 2 + core},
            )
        )
        sends[-1].start()

    if grid4:
        near, far, across = dst_chip(first), dst_chip(second), dst_chip(3)
        arrive(1)
        gathers[0].wait_recv()
        state = attend(chip)
        swap(0)
        accept_path(state)
        arrive(2)
        for forward in forwards:
            forward.wait_recv()
        for d in (1, 2):
            state = attend(src_chip(d))
            swap(d)
            accept_path(state)
        arrive(3)
        for d in (1, 2):
            swaps[d].wait_recv()
        add_up(near, 0, rows_dev, False)
        post(near, 1, 0, rows_dev, 1, first)
        forwards[2].wait_recv()
        state = attend(across)
        swap(3)
        swaps[3].wait_recv()
        for part in range(2):
            add_up(across, part * half, half, False)
            post(across, 3, part * half, half, 3 + part, first)
        relays = sends[1:3]
        accept_path(state)
        for part in range(2):
            relays[part].wait_recv()
            add_up(far, part * half, half, True)
            post(far, 2, part * half, half, (2, 5)[part], second)
        last = [sends[0], sends[3], sends[4]]
    else:
        gathers[0].wait_recv()
        for d in range(1, chips):
            arrive(d)
        for forward in forwards:
            forward.wait_recv()
        for p in range(pairs):
            accept_path(attend(p))
        for d in range(chips):
            swap(d)
        for d in range(1, chips):
            pair_and_send(d)
        last = sends

    swaps[0].wait_recv()
    for send in last:
        send.wait_recv()

    @pl.loop(0, rows_dev // 16)
    def _(i):
        at = pl.ds(pl.multiple_of(i * 16, 16), 16)
        total = terms[pl.ds(pl.multiple_of(own + i * 16, 16), 16), :].astype(F32)
        total = total + pair_in[chip, at, :].astype(F32)
        for d in range(1, 3 if grid4 else chips):
            total = total + rs_in[d, at, :].astype(F32)
        out[at, :] = (hidden[at, :].astype(F32) + total).astype(BF16)

    done = gathers[1] if grid4 else None
    for copy in [g for g in gathers if g is not done] + hops + forwards + list(swaps.values()) + sends:
        copy.wait_send()


def local(
    n,
    reps,
    hidden,
    norm_gain,
    w_query,
    w_key,
    w_value,
    w_output,
    kv_pool,
    page_table,
    cache_len,
    parents,
    depths,
    accept_node,
    migrate_to,
    leave_slot,
):
    slots, draft = parents.shape
    rows_dev, width = hidden.shape
    head = w_query.shape[1]
    count = slots * draft
    chips = n // 2
    vmem = pl.BlockSpec(memory_space=pltpu.VMEM)
    hbm = pl.BlockSpec(memory_space=pltpu.HBM)
    dma = pltpu.SemaphoreType.DMA
    page = kv_pool.shape[1]
    return pl.pallas_call(
        functools.partial(kernel, n, reps),
        out_shape=(
            jax.ShapeDtypeStruct((rows_dev, width), BF16),
            jax.ShapeDtypeStruct((slots, draft, 2 * head), BF16),
        ),
        in_specs=[vmem] * 3 + [hbm] * 2 + [pl.BlockSpec(memory_space=pl.ANY)] * 5 + [hbm] * 4,
        out_specs=(vmem, vmem),
        scratch_shapes=[
            pltpu.VMEM((count, width), BF16),
            pltpu.VMEM((width, 3 * head), BF16),
            pltpu.VMEM((width, head), BF16),
            pltpu.VMEM((kv_pool.shape[0] + 2 * reps, page, 2 * head), BF16),
            pltpu.VMEM((reps, 8, head), jnp.int32),
            pltpu.VMEM((slots, 1, head), jnp.int32),
            pltpu.VMEM((count, head), F32),
            pltpu.VMEM((count, head), F32),
            pltpu.VMEM((slots // 2, 2 * draft, 2 * draft), F32),
            pltpu.SMEM(page_table.shape, jnp.int32),
            pltpu.SMEM(cache_len.shape, jnp.int32),
            pltpu.SMEM(accept_node.shape, jnp.int32),
            pltpu.SMEM(migrate_to.shape, jnp.int32),
            pltpu.SMEM(leave_slot.shape, jnp.int32),
            pltpu.VMEM((slots // 2, 1, 2 * draft), jnp.int32),
            pltpu.VMEM((rows_dev, width), BF16),
            pltpu.VMEM(kv_pool.shape, BF16),
            pltpu.VMEM((head, width), BF16),
            pltpu.VMEM((count, width), BF16),
            pltpu.VMEM((chips, rows_dev, width), BF16),
            pltpu.VMEM((chips, rows_dev, width), BF16),
            pltpu.VMEM((chips, rows_dev, width), BF16),
            dma((12,)),
        ]
        + [dma((chips,))] * 6
        + [dma((chips + 2,))] * 2
        + [dma((reps,))] * 4,
        compiler_params=pltpu.CompilerParams(
            collective_id=0, has_side_effects=True, vmem_limit_bytes=60 * 1024 * 1024
        ),
    )(
        norm_gain,
        parents,
        depths,
        hidden,
        kv_pool,
        page_table,
        cache_len,
        accept_node,
        migrate_to,
        leave_slot,
        w_query,
        w_key,
        w_value,
        w_output,
    )


def solution(mesh):
    in_specs = (
        P(("rep", "tp"), None),
        P(),
        P(None, "tp"),
        P(None, "tp"),
        P(None, "tp"),
        P(None, "tp"),
        P("rep", None, "tp"),
        P("rep", None),
        P("rep"),
        P("rep", None),
        P("rep", None),
        P("rep"),
        P(),
        P(),
    )
    out_specs = (P(("rep", "tp"), None), P("rep", None, "tp"))
    fn = functools.partial(local, mesh.shape["tp"], mesh.shape["rep"])
    return jax.shard_map(fn, mesh=mesh, in_specs=in_specs, out_specs=out_specs, check_vma=False)
```
